512 devices in a mesh: req: 16 (over x, y), ctx: 32 (over z, core).
Axes of the slice: x: 4, y: 4, z: 16, core: 2. Of those that a mesh axis runs over, the one named last changes fastest.
Arguments:
- query: bfloat16 [2048, 4096], P(('req', 'ctx')), may hold values from -8 to 8
- prefix_id: int32 [2048], P('req'), may hold values from 0 to 31, as said below
- suffix_blocks: int32 [512, 4], P(('req', 'ctx')), may hold values from 1 to 2, 6 in all within a row
- prefix_kv: bfloat16 [32, 16384, 1024], P('ctx', 'req'), may hold values from -6 to 6
- suffix_kv: bfloat16 [2048, 256, 1024], P(('req', 'ctx')), may hold values from -8 to 8
- w_out: bfloat16 [4096, 5120], P('ctx', 'req'), may hold values from -0.046875 to 0.046875
Outputs:
- projected: bfloat16 [2048, 5120], P(('req', 'ctx'))
The draws below stay inside these ranges and needn't reach their ends.
Inputs may be any that keep to these rules, and one draw needn't show every extreme that they name: `prefix_id`: in each aligned block of 128 rows (one request group) the same two ids are named exactly 8 times, every other id at most 4 times, and the 4 rows of some one device all name one id. `suffix_blocks`: the 4 entries of one device sum to 6.
All inputs are finite; a program needn't handle non-finite values.
Results may differ from the reference program's by a relative error of at most 0.005.
Values may be sent and summed in bfloat16 or wider, within the bound.
No kernel may reach another device: no remote copies, remote signals or barrier semaphores. Data moves between devices by JAX's collectives and lax.ppermute only.
A program may use at most 64 MiB of HBM per device.

```python
import math
import jax
import jax.numpy as jnp
import numpy as np
from jax import lax

D = 5120
H = 32
KVH = 4
HD = 128
R_DEV = 4
PBLK = 1024
SB = 128
SBLK = 2
SMAX = 256
HQ = 4096
F2 = 1024
P_SIZE = 32
LP = 16384
GR = 128
ROWS = 2048
HOMES = 512


def draw_query(key, part):
    key = jax.random.fold_in(key, 3)
    values = jnp.clip(2.5 * jax.random.normal(key, (ROWS, HQ), jnp.float32), -8.0, 8.0)
    return values.astype(jnp.bfloat16)


def draw_prefix_kv(key, part):
    key = jax.random.fold_in(key, 5)
    drawn_table = jnp.clip(jax.random.normal(key, (P_SIZE, LP, F2), jnp.float32), -6.0, 6.0)
    return drawn_table.astype(jnp.bfloat16)


def draw_suffix_kv(key, part):
    key = jax.random.fold_in(key, 6)
    drawn_table = jnp.clip(1.5 * jax.random.normal(key, (ROWS, SMAX, F2), jnp.float32), -8.0, 8.0)
    return drawn_table.astype(jnp.bfloat16)


def draw_prefix_id(key, part):
    key = jax.random.fold_in(key, 7)
    popular = jax.random.permutation(jax.random.fold_in(key, 1), P_SIZE).astype(jnp.int32)
    remaining = popular[2:]
    tail_count = GR - 4 * R_DEV

    def one_group(group_index):
        group_key = jax.random.fold_in(jax.random.fold_in(key, 2), group_index)
        shuffle = jax.random.permutation(jax.random.fold_in(group_key, 1), P_SIZE - 2)
        tail_ids = remaining[shuffle][jnp.arange(tail_count) % (P_SIZE - 2)]
        anchor = jnp.full((R_DEV,), popular[0], jnp.int32)
        pooled = jnp.concatenate([anchor, jnp.full((2 * R_DEV,), popular[1], jnp.int32), tail_ids])
        pooled = jax.random.permutation(jax.random.fold_in(group_key, 2), pooled)
        offset = jax.random.randint(jax.random.fold_in(group_key, 3), (), 0, GR // R_DEV) * R_DEV
        return jnp.roll(jnp.concatenate([anchor, pooled]), offset)
    return jax.vmap(one_group)(jnp.arange(ROWS // GR)).reshape(ROWS).astype(jnp.int32)


def steps_of(rng, dims, split, smallest, high):
    factor_of = 1.0
    for axis_at, parts in split:
        draws = jax.random.uniform(jax.random.fold_in(jax.random.fold_in(rng, 6), axis_at), (parts,), jnp.float32, smallest / len(split), high / len(split))
        factor_of = factor_of * jnp.repeat(jnp.exp(draws), dims[axis_at] // parts).reshape((-1,) + (1,) * (len(dims) - 1 - axis_at))
    return factor_of


def profile(number_of, total, reach, lean):
    loads = [(1 << 20) // math.isqrt(standing ** lean) + 1 for standing in range(2, number_of + 1)]
    spare, counts = total - reach - (number_of - 1), [1] * (number_of - 1)
    while spare > 0:
        free = [i for i in range(number_of - 1) if counts[i] < reach]
        whole, left = sum([loads[i] for i in free]), spare
        for i in free:
            extra = min(reach - counts[i], max(1, left * loads[i] // whole), spare)
            counts[i] = counts[i] + extra
            spare = spare - extra
    return np.array([reach] + counts)


def uneven_parts(own_key, amount, total, reach, skew):
    if amount == 2:
        one = jax.random.randint(own_key, (), max(1, total - reach), min(reach, total - 1) + 1)
        return jnp.stack([one, total - one])
    sizes = jnp.asarray(profile(amount, total, reach, skew), jnp.int32)
    couples = (amount - 1) // 2
    donor, sink = sizes[1:1 + 2 * couples:2], sizes[2:2 + 2 * couples:2]
    room = jnp.minimum(donor - 1, reach - sink)
    shifted = jax.random.randint(jax.random.fold_in(own_key, 1), (couples,), 0, 1 << 20) % (room + 1)
    sizes = sizes.at[1:1 + 2 * couples:2].set(donor - shifted).at[2:2 + 2 * couples:2].set(sink + shifted)
    return sizes[jax.random.permutation(jax.random.fold_in(own_key, 2), amount)]


def bell_draw(stream_key, dims, scale, reach, shards=(), held_as=jnp.bfloat16):
    values = scale * jax.random.normal(stream_key, dims, jnp.float32)
    if shards:
        values = values * steps_of(stream_key, dims, shards, -0.22, 0.18)
    return jnp.clip(values, -reach, reach).astype(held_as)


def setup_inputs(seed: int = 0) -> dict:
    keys = jax.random.split(jax.random.key(seed), 7)
    query = draw_query(jax.random.fold_in(keys[6], 71), 0)
    prefix_id = draw_prefix_id(jax.random.fold_in(keys[6], 71), 0)
    suffix_blocks = jax.vmap(lambda own: uneven_parts(own, R_DEV, 3 * R_DEV // 2, SBLK, 0))(jax.random.split(keys[2], HOMES)).reshape((HOMES, R_DEV)).astype(jnp.int32)
    prefix_kv = draw_prefix_kv(jax.random.fold_in(keys[6], 71), 0)
    suffix_kv = draw_suffix_kv(jax.random.fold_in(keys[6], 71), 0)
    w_out = bell_draw(keys[5], (HQ, D), (4 * HQ) ** -0.5, 0.046875, ((0, 32), (1, 16)))
    return dict(query=query, prefix_id=prefix_id, suffix_blocks=suffix_blocks, prefix_kv=prefix_kv, suffix_kv=suffix_kv, w_out=w_out)


NEGATIVE = -1.0e30
HIGH = lax.Precision.HIGHEST


def soft_attend(scores, value_rows, form):
    maxima = jnp.max(scores, axis=-1, keepdims=True)
    expo = jnp.exp(scores - maxima)
    summed = jnp.sum(expo, axis=-1, keepdims=True)
    weights = lax.optimization_barrier(expo.astype(jnp.bfloat16)).astype(jnp.float32)
    output = jnp.einsum(form, weights, value_rows, precision=HIGH) / summed
    return output, maxima[..., 0] + jnp.log(summed[..., 0])


def row_attention(row_query, prefix_rows, suffix_rows, length):
    factor = HD ** -0.5
    group_size = H // KVH
    key_width = KVH * HD
    shaped = row_query.reshape(KVH, group_size, HD).astype(jnp.float32)
    prefix_keys = prefix_rows[:, :key_width].reshape(LP // PBLK, PBLK, KVH, HD).astype(jnp.float32)
    prefix_values = prefix_rows[:, key_width:].reshape(LP // PBLK, PBLK, KVH, HD).astype(jnp.float32)
    scores = jnp.einsum("kgd,btkd->bkgt", shaped, prefix_keys, precision=HIGH) * factor
    block_out, block_log = soft_attend(scores, prefix_values, "bkgt,btkd->bkgd")
    peak = jnp.max(block_log, axis=0)
    factors = jnp.exp(block_log - peak)
    summed = jnp.sum(factors, axis=0)
    prefix_out = jnp.sum(factors[..., None] * block_out, axis=0) / summed[..., None]
    prefix_log = peak + jnp.log(summed)
    suffix_keys = suffix_rows[:, :key_width].reshape(SMAX, KVH, HD).astype(jnp.float32)
    suffix_values = suffix_rows[:, key_width:].reshape(SMAX, KVH, HD).astype(jnp.float32)
    scores = jnp.einsum("kgd,skd->kgs", shaped, suffix_keys, precision=HIGH) * factor
    live = jnp.arange(SMAX, dtype=jnp.int32) < length
    scores = jnp.where(live[None, None, :], scores, NEGATIVE)
    suffix_out, suffix_log = soft_attend(scores, suffix_values, "kgs,skd->kgd")
    top_log = jnp.maximum(prefix_log, suffix_log)
    prefix_weight = jnp.exp(prefix_log - top_log)[..., None]
    suffix_weight = jnp.exp(suffix_log - top_log)[..., None]
    mixed = (prefix_weight * prefix_out + suffix_weight * suffix_out) / (prefix_weight + suffix_weight)
    return mixed.reshape(H * HD).astype(jnp.bfloat16)


def reference(query, prefix_id, suffix_blocks, prefix_kv, suffix_kv, w_out):
    lengths = (suffix_blocks.reshape(ROWS) * SB).astype(jnp.int32)

    def one_row(operands):
        row_query, prefix_index, suffix_rows, length = operands
        prefix_rows = lax.dynamic_index_in_dim(prefix_kv, prefix_index.astype(jnp.int32), 0, keepdims=False)
        return row_attention(row_query, prefix_rows, suffix_rows, length)

    attention = lax.map(one_row, (query, prefix_id, suffix_kv, lengths))
    return jnp.dot(attention, w_out, preferred_element_type=jnp.float32).astype(jnp.bfloat16)
```

```python
import functools

import jax
import jax.numpy as jnp
from jax import lax
from jax.experimental import pallas as pl
from jax.experimental.pallas import tpu as pltpu
from jax.sharding import PartitionSpec as P

KVH = 4
HD = 128
SB = 128
SLOTS = 8
GROUP = 8
FACTOR = HD**-0.5
LOG2E = 1.4426950408889634
NEGATIVE = -1e30
BF16 = jnp.bfloat16
F32 = jnp.float32


def split3(x):
    high = lax.reduce_precision(x, 8, 7)
    rest = x - high
    middle = lax.reduce_precision(rest, 8, 7)
    return high.astype(BF16), middle.astype(BF16), (rest - middle).astype(BF16)


def attention_kernel(q_ref, k_ref, v_ref, out_ref, parts_ref):
    head = pl.program_id(0)
    groups, rows, _ = q_ref.shape
    total = groups * rows
    tile = min(256, total)
    keys = k_ref[...]
    values = v_ref[...].T
    queries = q_ref[...].reshape(total, HD)

    @pl.when(head == 0)
    def _():
        parts_ref[...] = jnp.zeros_like(parts_ref)

    per = tile // rows
    for at in range(total // tile):
        scores = lax.dot_general(
            keys, queries[at * tile : (at + 1) * tile], (((1,), (1,)), ((), ())),
            preferred_element_type=F32,
        )
        top = jnp.max(scores, axis=0, keepdims=True)
        expo = jnp.exp2((scores - top) * (FACTOR * LOG2E))
        summed = jnp.sum(expo, axis=0, keepdims=True)
        output = jnp.dot(values, expo.astype(BF16), preferred_element_type=F32) / summed
        out_ref[at * per : (at + 1) * per, pl.ds(pl.multiple_of(head * rows, rows), rows), :] = (
            output.T.astype(BF16).reshape(per, rows, HD)
        )
        lse = top * FACTOR + jnp.log(summed)
        high = lse.astype(BF16).astype(F32)
        rest = lse - high
        middle = rest.astype(BF16).astype(F32)
        cols = slice(at * tile, (at + 1) * tile)
        parts_ref[pl.ds(head, 1), cols] = high
        parts_ref[pl.ds(KVH + head, 1), cols] = middle
        parts_ref[pl.ds(2 * KVH + head, 1), cols] = rest - middle

    @pl.when(head == KVH - 1)
    def _():
        whole = parts_ref[...]
        rolled = pltpu.roll(whole, total - rows, 1)
        for r in range(groups):
            source = whole if r % 2 == 0 else rolled
            at = r // 2 * 128
            out_ref[r, KVH * rows :, :] = source[:, at : at + 128].astype(BF16)


def prefix_attention(queries, kv):
    groups, rows, _ = queries.shape
    tokens = kv.shape[0]
    each = rows // KVH
    return pl.pallas_call(
        attention_kernel,
        out_shape=jax.ShapeDtypeStruct((groups, rows + 16, HD), BF16),
        grid=(KVH,),
        in_specs=[
            pl.BlockSpec((groups, each, HD), lambda h: (0, h, 0)),
            pl.BlockSpec((tokens, HD), lambda h: (0, h)),
            pl.BlockSpec((tokens, HD), lambda h: (0, KVH + h)),
        ],
        out_specs=pl.BlockSpec((groups, rows + 16, HD), lambda h: (0, 0, 0)),
        scratch_shapes=[pltpu.VMEM((16, groups * each), F32)],
        compiler_params=pltpu.CompilerParams(vmem_limit_bytes=48 * 2**20),
        cost_estimate=pl.CostEstimate(
            flops=4 * groups * rows * tokens * HD,
            bytes_accessed=4 * groups * rows * HD + 4 * tokens * KVH * HD,
            transcendentals=groups * rows * tokens,
        ),
    )(queries, kv, kv)


def suffix_attention(query, suffix_kv, lengths):
    rows = query.shape[0]
    positions = suffix_kv.shape[1]
    shaped = query.reshape(rows, KVH, -1, HD)
    keys = suffix_kv[:, :, : KVH * HD].reshape(rows, positions, KVH, HD)
    values = suffix_kv[:, :, KVH * HD :].reshape(rows, positions, KVH, HD)
    scores = jnp.einsum("rkgd,rskd->rkgs", shaped, keys, preferred_element_type=F32) * FACTOR
    live = jnp.arange(positions, dtype=jnp.int32)[None, :] < lengths[:, None]
    scores = jnp.where(live[:, None, None, :], scores, NEGATIVE)
    top = jnp.max(scores, axis=-1, keepdims=True)
    expo = jnp.exp(scores - top)
    summed = jnp.sum(expo, axis=-1, keepdims=True)
    output = (
        jnp.einsum("rkgs,rskd->rkgd", expo.astype(BF16), values, preferred_element_type=F32)
        / summed
    )
    lse = top + jnp.log(summed)
    return output.reshape(rows, -1, HD), lse.reshape(rows, -1, 1)


def a2a(x, axis, groups=None):
    return lax.all_to_all(x, axis, 0, 0, tiled=True, axis_index_groups=groups)


def local(query, prefix_id, suffix_blocks, prefix_kv, suffix_kv, w_out):
    req = lax.axis_size("req")
    ctx = lax.axis_size("ctx")
    rows = query.shape[0]
    heads = query.shape[1] // HD
    group_rows = rows * ctx
    slots = ctx * SLOTS
    near = [list(range(a, a + GROUP)) for a in range(0, ctx, GROUP)]
    width = w_out.shape[1] // GROUP

    with jax.named_scope("weights"):
        block = w_out.T.reshape(GROUP, width, HD)
        block = a2a(block, "ctx", near).transpose(1, 0, 2).reshape(width, GROUP * HD)
        weights = lax.all_gather(block, "req", axis=0, tiled=True)

    with jax.named_scope("suffix"):
        suffix_out, suffix_lse = suffix_attention(query, suffix_kv, suffix_blocks[0] * SB)

    with jax.named_scope("query_to_heads"):
        payload = jnp.concatenate(
            [
                query.reshape(rows, heads, HD),
                suffix_out.astype(BF16),
                *split3(suffix_lse),
                jnp.zeros((rows, heads, HD - 3), BF16),
            ],
            axis=-1,
        )
        by_head = a2a(payload.transpose(1, 0, 2), "ctx").reshape(group_rows, 3 * HD)

    with jax.named_scope("heads_to_slots"):
        index = jnp.arange(group_rows, dtype=jnp.int32)
        same = prefix_id[:, None] == prefix_id[None, :]
        rank = jnp.sum((same & (index[None, :] < index[:, None])).astype(jnp.int32), axis=1)
        slot = prefix_id * SLOTS + rank
        place = (slot[None, :] == jnp.arange(slots, dtype=jnp.int32)[:, None]).astype(BF16)
        picked = jnp.dot(place, by_head[:, :HD], preferred_element_type=F32).astype(BF16)
        by_slot = a2a(picked.reshape(ctx, SLOTS, HD), "ctx").reshape(heads * SLOTS, HD)

    with jax.named_scope("gather_req"):
        spread = jnp.broadcast_to(by_slot[None], (req, *by_slot.shape))
        gathered = a2a(spread, "req")

    with jax.named_scope("prefix"):
        partials = prefix_attention(gathered, prefix_kv[0])
        received = a2a(partials, "req")

    with jax.named_scope("merge"):
        count = heads * SLOTS
        logs = received[:, count : count + 3 * KVH, : count // KVH].astype(F32)
        logs = jnp.sum(logs.reshape(req, 3, count), axis=1)
        peak = jnp.max(logs, axis=0)
        shares = jnp.exp(logs - peak)
        total = jnp.sum(shares, axis=0)
        merged = jnp.sum(shares[..., None] * received[:, :count].astype(F32), axis=0)
        merged = (merged / total[:, None]).astype(BF16)
        merged_lse = (peak + jnp.log(total))[:, None]

    with jax.named_scope("slots_to_heads"):
        payload = jnp.concatenate(
            [merged, *split3(merged_lse), jnp.zeros((count, HD - 3), BF16)], axis=-1
        )
        arrived = a2a(payload.reshape(heads, SLOTS, 2 * HD), "ctx").reshape(slots, 2 * HD)

    with jax.named_scope("mix"):
        prefix = lax.dot_general(
            place, arrived, (((0,), (0,)), ((), ())), preferred_element_type=F32
        )
        prefix_lse = jnp.sum(prefix[:, HD : HD + 3], axis=1, keepdims=True)
        own = by_head[:, HD:].astype(F32)
        own_lse = jnp.sum(own[:, HD : HD + 3], axis=1, keepdims=True)
        top = jnp.maximum(prefix_lse, own_lse)
        prefix_share = jnp.exp(prefix_lse - top)
        own_share = jnp.exp(own_lse - top)
        attention = (prefix_share * prefix[:, :HD] + own_share * own[:, :HD]) / (
            prefix_share + own_share
        )
        attention = attention.astype(BF16)

    with jax.named_scope("projection"):
        shared = a2a(jnp.broadcast_to(attention[None], (GROUP, *attention.shape)), "ctx", near)
        shared = shared.transpose(1, 0, 2).reshape(group_rows, GROUP * HD)
        terms = lax.dot_general(
            shared, weights, (((1,), (1,)), ((), ())), preferred_element_type=F32
        ).astype(BF16)
        home = a2a(terms.reshape(ctx, rows, -1), "ctx")
        home = home.reshape(ctx // GROUP, GROUP, rows, req, width).astype(F32)
        summed = jnp.sum(home, axis=0).transpose(1, 2, 0, 3)
        return summed.reshape(rows, -1).astype(BF16)


def solution(mesh):
    in_specs = (
        P(("req", "ctx"), None),
        P("req"),
        P(("req", "ctx"), None),
        P("ctx", "req", None),
        P(("req", "ctx"), None, None),
        P("ctx", "req"),
    )
    out_specs = P(("req", "ctx"), None)
    return jax.shard_map(local, mesh=mesh, in_specs=in_specs, out_specs=out_specs, check_vma=False)
```

```python
import functools

import jax
import jax.numpy as jnp
from jax import lax
from jax.experimental import pallas as pl
from jax.experimental.pallas import tpu as pltpu
from jax.sharding import PartitionSpec as P

KVH = 4
HD = 128
SB = 128
SLOTS = 8
GROUP = 8
TILE = 128
FACTOR = HD**-0.5
LOG2E = 1.4426950408889634
NEGATIVE = -1e30
BF16 = jnp.bfloat16
F32 = jnp.float32


def split3(x):
    high = lax.reduce_precision(x, 8, 7)
    rest = x - high
    middle = lax.reduce_precision(rest, 8, 7)
    return high.astype(BF16), middle.astype(BF16), (rest - middle).astype(BF16)


def attention_kernel(q_ref, k_ref, v_ref, out_ref, lse_ref):
    head = pl.program_id(0)
    groups, rows, _ = q_ref.shape
    total = groups * rows
    keys = k_ref[...]
    values = jnp.concatenate([v_ref[...], jnp.ones((v_ref.shape[0], HD), BF16)], axis=1)
    per = TILE // rows

    def score(at):
        queries = q_ref[at * per : (at + 1) * per].reshape(TILE, HD)
        return lax.dot_general(
            queries, keys, (((1,), (1,)), ((), ())), preferred_element_type=F32
        )

    following = score(0)
    for at in range(total // TILE):
        scores = following
        if (at + 1) * TILE < total:
            following = score(at + 1)
        top = jnp.max(scores, axis=1, keepdims=True)
        weights = jnp.exp2((scores - top) * (FACTOR * LOG2E)).astype(BF16)
        both = jnp.dot(weights, values, preferred_element_type=F32)
        summed = both[:, HD:]
        out_ref[at * per : (at + 1) * per, pl.ds(pl.multiple_of(head * rows, rows), rows), :] = (
            (both[:, :HD] / summed).astype(BF16).reshape(per, rows, HD)
        )
        lse = top * FACTOR + jnp.log(summed)
        for j in range(TILE // 128):
            lse_ref[
                pl.ds(pl.multiple_of(head * 8, 8), 8),
                at * TILE + 128 * j : at * TILE + 128 * j + 128,
            ] = lse[128 * j : 128 * j + 128].T[0:8]

    @pl.when(head == KVH - 1)
    def _():
        row = lax.broadcasted_iota(jnp.int32, (8, total), 0)
        upper = jnp.zeros((8, total), F32)
        lower = upper
        for h in range(KVH):
            whole = lse_ref[8 * h : 8 * h + 8, :]
            high = whole.astype(BF16).astype(F32)
            rest = whole - high
            middle = rest.astype(BF16).astype(F32)
            upper = jnp.where(row == h, high, jnp.where(row == KVH + h, middle, upper))
            lower = jnp.where(row == h, rest - middle, lower)
        parts = jnp.concatenate([upper, lower], axis=0)
        rolled = pltpu.roll(parts, total - rows, 1)
        for r in range(groups):
            source = parts if r % 2 == 0 else rolled
            at = r // 2 * 128
            out_ref[r, KVH * rows :, :] = source[:, at : at + 128].astype(BF16)


def prefix_attention(queries, kv):
    groups, rows, _ = queries.shape
    tokens = kv.shape[0]
    each = rows // KVH
    return pl.pallas_call(
        attention_kernel,
        out_shape=jax.ShapeDtypeStruct((groups, rows + 16, HD), BF16),
        grid=(KVH,),
        in_specs=[
            pl.BlockSpec((groups, each, HD), lambda h: (0, h, 0)),
            pl.BlockSpec((tokens, HD), lambda h: (0, h)),
            pl.BlockSpec((tokens, HD), lambda h: (0, KVH + h)),
        ],
        out_specs=pl.BlockSpec((groups, rows + 16, HD), lambda h: (0, 0, 0)),
        scratch_shapes=[pltpu.VMEM((8 * KVH, groups * each), F32)],
        compiler_params=pltpu.CompilerParams(vmem_limit_bytes=48 * 2**20),
        cost_estimate=pl.CostEstimate(
            flops=4 * groups * rows * tokens * HD,
            bytes_accessed=4 * groups * rows * HD + 4 * tokens * KVH * HD,
            transcendentals=groups * rows * tokens,
        ),
    )(queries, kv, kv)


def suffix_attention(query, suffix_kv, lengths):
    rows = query.shape[0]
    positions = suffix_kv.shape[1]
    shaped = query.reshape(rows, KVH, -1, HD)
    keys = suffix_kv[:, :, : KVH * HD].reshape(rows, positions, KVH, HD)
    values = suffix_kv[:, :, KVH * HD :].reshape(rows, positions, KVH, HD)
    scores = jnp.einsum("rkgd,rskd->rkgs", shaped, keys, preferred_element_type=F32) * FACTOR
    live = jnp.arange(positions, dtype=jnp.int32)[None, :] < lengths[:, None]
    scores = jnp.where(live[:, None, None, :], scores, NEGATIVE)
    top = jnp.max(scores, axis=-1, keepdims=True)
    expo = jnp.exp(scores - top)
    summed = jnp.sum(expo, axis=-1, keepdims=True)
    output = (
        jnp.einsum("rkgs,rskd->rkgd", expo.astype(BF16), values, preferred_element_type=F32)
        / summed
    )
    lse = top + jnp.log(summed)
    return output.reshape(rows, -1, HD), lse.reshape(rows, -1, 1)


def a2a(x, axis, groups=None):
    return lax.all_to_all(x, axis, 0, 0, tiled=True, axis_index_groups=groups)


def local(query, prefix_id, suffix_blocks, prefix_kv, suffix_kv, w_out):
    req = lax.axis_size("req")
    ctx = lax.axis_size("ctx")
    rows = query.shape[0]
    heads = query.shape[1] // HD
    group_rows = rows * ctx
    slots = ctx * SLOTS
    near = [list(range(a, a + GROUP)) for a in range(0, ctx, GROUP)]
    far = [list(range(m, ctx, GROUP)) for m in range(GROUP)]
    width = w_out.shape[1] // GROUP
    share = heads // GROUP
    count = heads * SLOTS
    mine = lax.axis_index("ctx") // GROUP

    with jax.named_scope("split_near"):
        asked = query.reshape(rows, GROUP, share, HD).transpose(1, 2, 0, 3)
        asked = asked.reshape(GROUP, share * rows, HD)
        payload = jnp.concatenate([asked, w_out.T.reshape(GROUP, width, HD)], axis=1)
        payload = a2a(payload, "ctx", near)
        asked = payload[:, : share * rows]
        block = payload[:, share * rows :].transpose(1, 0, 2).reshape(width, GROUP * HD)

    with jax.named_scope("weights"):
        weights = lax.all_gather(block, "req", axis=0, tiled=True)

    with jax.named_scope("gather_far"):
        asked = lax.all_gather(asked, "ctx", axis=0, tiled=True, axis_index_groups=far)
        asked = asked.reshape(ctx, share, rows, HD).transpose(0, 2, 1, 3)
        asked = asked.reshape(group_rows, share * HD)

    with jax.named_scope("slots"):
        index = jnp.arange(group_rows, dtype=jnp.int32)
        same = prefix_id[:, None] == prefix_id[None, :]
        rank = jnp.sum((same & (index[None, :] < index[:, None])).astype(jnp.int32), axis=1)
        slot = prefix_id * SLOTS + rank
        close = jnp.arange(GROUP * SLOTS, dtype=jnp.int32) + mine * (GROUP * SLOTS)
        place = (slot[None, :] == close[:, None]).astype(BF16)
        picked = jnp.dot(place, asked, preferred_element_type=F32).astype(BF16)
        picked = picked.reshape(GROUP, SLOTS, share, HD).transpose(0, 2, 1, 3)
        by_slot = a2a(picked, "ctx", near).reshape(count, HD)

    with jax.named_scope("gather_req"):
        spread = jnp.broadcast_to(by_slot[None], (req, *by_slot.shape))
        gathered = a2a(spread, "req")

    with jax.named_scope("prefix"):
        partials = prefix_attention(gathered, prefix_kv[0])
        received = a2a(partials, "req")

    with jax.named_scope("suffix"):
        own, own_lse = suffix_attention(query, suffix_kv, suffix_blocks[0] * SB)
        own = own.astype(BF16).transpose(1, 0, 2)
        own_lse = own_lse[..., 0].T

    with jax.named_scope("merge"):
        logs = received[:, count : count + 3 * KVH, : count // KVH].astype(F32)
        logs = jnp.sum(logs.reshape(req, 3, count), axis=1)
        peak = jnp.max(logs, axis=0)
        shares = jnp.exp(logs - peak)
        total = jnp.sum(shares, axis=0)
        merged = jnp.sum(shares[..., None] * received[:, :count].astype(F32), axis=0)
        merged = (merged / total[:, None]).astype(BF16)
        merged_lse = (peak + jnp.log(total)).reshape(heads, SLOTS)

    with jax.named_scope("to_heads"):
        each = SLOTS + rows
        parts = jnp.concatenate(split3(jnp.concatenate([merged_lse, own_lse], axis=1)), axis=1)
        parts = jnp.pad(parts, ((0, 0), (0, HD - 3 * each)))[:, None]
        payload = jnp.concatenate(
            [merged.reshape(heads, SLOTS, HD), own, parts, jnp.zeros((heads, 3, HD), BF16)], axis=1
        )
        arrived = a2a(payload, "ctx")

    with jax.named_scope("mix"):
        match = slot[:, None] == jnp.arange(slots, dtype=jnp.int32)[None, :]
        prefix = jnp.dot(
            match.astype(BF16), arrived[:, :SLOTS].reshape(slots, HD), preferred_element_type=F32
        )
        logs = arrived[:, each, : 3 * each].astype(F32).reshape(ctx, 3, each).sum(axis=1)
        prefix_lse = jnp.sum(
            jnp.where(match, logs[:, :SLOTS].reshape(1, slots), 0.0), axis=1, keepdims=True
        )
        own = arrived[:, SLOTS:each].astype(F32).reshape(group_rows, HD)
        own_lse = logs[:, SLOTS:].reshape(group_rows, 1)
        top = jnp.maximum(prefix_lse, own_lse)
        prefix_share = jnp.exp(prefix_lse - top)
        own_share = jnp.exp(own_lse - top)
        attention = (prefix_share * prefix + own_share * own) / (prefix_share + own_share)
        attention = attention.astype(BF16)

    with jax.named_scope("projection"):
        shared = a2a(jnp.broadcast_to(attention[None], (GROUP, *attention.shape)), "ctx", near)
        shared = shared.transpose(1, 0, 2).reshape(group_rows, GROUP * HD)
        terms = lax.dot_general(
            shared, weights, (((1,), (1,)), ((), ())), preferred_element_type=F32
        ).astype(BF16)
        home = a2a(terms.reshape(ctx, rows, -1), "ctx")
        home = home.reshape(ctx // GROUP, GROUP, rows, req, width).astype(F32)
        summed = jnp.sum(home, axis=0).transpose(1, 2, 0, 3)
        return summed.reshape(rows, -1).astype(BF16)


def solution(mesh):
    in_specs = (
        P(("req", "ctx"), None),
        P("req"),
        P(("req", "ctx"), None),
        P("ctx", "req", None),
        P(("req", "ctx"), None, None),
        P("ctx", "req"),
    )
    out_specs = P(("req", "ctx"), None)
    return jax.shard_map(local, mesh=mesh, in_specs=in_specs, out_specs=out_specs, check_vma=False)
```

```python
import functools

import jax
import jax.numpy as jnp
from jax import lax
from jax.experimental import pallas as pl
from jax.experimental.pallas import tpu as pltpu
from jax.sharding import PartitionSpec as P

KVH = 4
HD = 128
SB = 128
SLOTS = 8
GROUP = 8
TILE = 128
FACTOR = HD**-0.5
LOG2E = 1.4426950408889634
NEGATIVE = -1e30
BF16 = jnp.bfloat16
F32 = jnp.float32


def split3(x):
    high = lax.reduce_precision(x, 8, 7)
    rest = x - high
    middle = lax.reduce_precision(rest, 8, 7)
    return high.astype(BF16), middle.astype(BF16), (rest - middle).astype(BF16)


def attention_kernel(q_ref, k_ref, v_ref, out_ref, lse_ref):
    head = pl.program_id(0)
    groups, rows, _ = q_ref.shape
    total = groups * rows
    keys = k_ref[...]
    values = jnp.concatenate([v_ref[...], jnp.ones((v_ref.shape[0], HD), BF16)], axis=1)
    per = TILE // rows

    def score(at):
        queries = q_ref[at * per : (at + 1) * per].reshape(TILE, HD)
        return lax.dot_general(
            queries, keys, (((1,), (1,)), ((), ())), preferred_element_type=F32
        )

    following = score(0)
    for at in range(total // TILE):
        scores = following
        if (at + 1) * TILE < total:
            following = score(at + 1)
        top = jnp.max(scores, axis=1, keepdims=True)
        weights = jnp.exp2((scores - top) * (FACTOR * LOG2E)).astype(BF16)
        both = jnp.dot(weights, values, preferred_element_type=F32)
        summed = both[:, HD:]
        out_ref[at * per : (at + 1) * per, pl.ds(pl.multiple_of(head * rows, rows), rows), :] = (
            (both[:, :HD] / summed).astype(BF16).reshape(per, rows, HD)
        )
        lse = top * FACTOR + jnp.log(summed)
        for j in range(TILE // 128):
            lse_ref[
                pl.ds(pl.multiple_of(head * 8, 8), 8),
                at * TILE + 128 * j : at * TILE + 128 * j + 128,
            ] = lse[128 * j : 128 * j + 128].T[0:8]

    @pl.when(head == KVH - 1)
    def _():
        row = lax.broadcasted_iota(jnp.int32, (8, total), 0)
        upper = jnp.zeros((8, total), F32)
        lower = upper
        for h in range(KVH):
            whole = lse_ref[8 * h : 8 * h + 8, :]
            high = whole.astype(BF16).astype(F32)
            rest = whole - high
            middle = rest.astype(BF16).astype(F32)
            upper = jnp.where(row == h, high, jnp.where(row == KVH + h, middle, upper))
            lower = jnp.where(row == h, rest - middle, lower)
        parts = jnp.concatenate([upper, lower], axis=0)
        rolled = pltpu.roll(parts, total - rows, 1)
        for r in range(groups):
            source = parts if r % 2 == 0 else rolled
            at = r // 2 * 128
            out_ref[r, KVH * rows :, :] = source[:, at : at + 128].astype(BF16)


def prefix_attention(queries, kv):
    groups, rows, _ = queries.shape
    tokens = kv.shape[0]
    each = rows // KVH
    return pl.pallas_call(
        attention_kernel,
        out_shape=jax.ShapeDtypeStruct((groups, rows + 16, HD), BF16),
        grid=(KVH,),
        in_specs=[
            pl.BlockSpec((groups, each, HD), lambda h: (0, h, 0)),
            pl.BlockSpec((tokens, HD), lambda h: (0, h)),
            pl.BlockSpec((tokens, HD), lambda h: (0, KVH + h)),
        ],
        out_specs=pl.BlockSpec((groups, rows + 16, HD), lambda h: (0, 0, 0)),
        scratch_shapes=[pltpu.VMEM((8 * KVH, groups * each), F32)],
        compiler_params=pltpu.CompilerParams(vmem_limit_bytes=48 * 2**20),
        cost_estimate=pl.CostEstimate(
            flops=4 * groups * rows * tokens * HD,
            bytes_accessed=4 * groups * rows * HD + 4 * tokens * KVH * HD,
            transcendentals=groups * rows * tokens,
        ),
    )(queries, kv, kv)


def suffix_attention(query, suffix_kv, lengths):
    rows = query.shape[0]
    positions = suffix_kv.shape[1]
    shaped = query.reshape(rows, KVH, -1, HD)
    keys = suffix_kv[:, :, : KVH * HD].reshape(rows, positions, KVH, HD)
    values = suffix_kv[:, :, KVH * HD :].reshape(rows, positions, KVH, HD)
    scores = jnp.einsum("rkgd,rskd->rkgs", shaped, keys, preferred_element_type=F32) * FACTOR
    live = jnp.arange(positions, dtype=jnp.int32)[None, :] < lengths[:, None]
    scores = jnp.where(live[:, None, None, :], scores, NEGATIVE)
    top = jnp.max(scores, axis=-1, keepdims=True)
    expo = jnp.exp(scores - top)
    summed = jnp.sum(expo, axis=-1, keepdims=True)
    output = (
        jnp.einsum("rkgs,rskd->rkgd", expo.astype(BF16), values, preferred_element_type=F32)
        / summed
    )
    lse = top + jnp.log(summed)
    return output.reshape(rows, -1, HD), lse.reshape(rows, -1, 1)


def a2a(x, axis, groups=None):
    return lax.all_to_all(x, axis, 0, 0, tiled=True, axis_index_groups=groups)


def local(query, prefix_id, suffix_blocks, prefix_kv, suffix_kv, w_out):
    req = lax.axis_size("req")
    ctx = lax.axis_size("ctx")
    rows = query.shape[0]
    heads = query.shape[1] // HD
    group_rows = rows * ctx
    slots = ctx * SLOTS
    near = [list(range(a, a + GROUP)) for a in range(0, ctx, GROUP)]
    far = [list(range(m, ctx, GROUP)) for m in range(GROUP)]
    width = w_out.shape[1] // GROUP
    share = heads // GROUP
    count = heads * SLOTS
    mine = lax.axis_index("ctx") // GROUP

    with jax.named_scope("split_near"):
        asked = query.reshape(rows, GROUP, share, HD).transpose(1, 2, 0, 3)
        asked = asked.reshape(GROUP, share * rows, HD)
        payload = jnp.concatenate([asked, w_out.T.reshape(GROUP, width, HD)], axis=1)
        payload = a2a(payload, "ctx", near)
        asked = payload[:, : share * rows]
        block = payload[:, share * rows :].transpose(1, 0, 2).reshape(width, GROUP * HD)

    with jax.named_scope("weights"):
        weights = lax.all_gather(block, "req", axis=0, tiled=True)

    with jax.named_scope("gather_far"):
        asked = lax.all_gather(asked, "ctx", axis=0, tiled=True, axis_index_groups=far)
        asked = asked.reshape(ctx, share, rows, HD).transpose(0, 2, 1, 3)
        asked = asked.reshape(group_rows, share * HD)

    with jax.named_scope("slots"):
        index = jnp.arange(group_rows, dtype=jnp.int32)
        same = prefix_id[:, None] == prefix_id[None, :]
        rank = jnp.sum((same & (index[None, :] < index[:, None])).astype(jnp.int32), axis=1)
        slot = prefix_id * SLOTS + rank
        close = jnp.arange(GROUP * SLOTS, dtype=jnp.int32) + mine * (GROUP * SLOTS)
        place = (slot[None, :] == close[:, None]).astype(BF16)
        picked = jnp.dot(place, asked, preferred_element_type=F32).astype(BF16)
        picked = picked.reshape(GROUP, SLOTS, share, HD).transpose(0, 2, 1, 3)
        by_slot = a2a(picked, "ctx", near).reshape(count, HD)

    with jax.named_scope("gather_req"):
        spread = jnp.broadcast_to(by_slot[None], (req, *by_slot.shape))
        gathered = a2a(spread, "req")

    with jax.named_scope("prefix"):
        partials = prefix_attention(gathered, prefix_kv[0])
        partials, weights = lax.optimization_barrier((partials, weights))
        received = a2a(partials, "req")

    with jax.named_scope("suffix"):
        own, own_lse = suffix_attention(query, suffix_kv, suffix_blocks[0] * SB)
        own = own.astype(BF16).transpose(1, 0, 2)
        own_lse = own_lse[..., 0].T

    with jax.named_scope("merge"):
        logs = received[:, count : count + 3 * KVH, : count // KVH].astype(F32)
        logs = jnp.sum(logs.reshape(req, 3, count), axis=1)
        peak = jnp.max(logs, axis=0)
        shares = jnp.exp(logs - peak)
        total = jnp.sum(shares, axis=0)
        merged = jnp.sum(shares[..., None] * received[:, :count].astype(F32), axis=0)
        merged = (merged / total[:, None]).astype(BF16)
        merged_lse = (peak + jnp.log(total)).reshape(heads, SLOTS)

    with jax.named_scope("to_heads"):
        each = SLOTS + rows
        parts = jnp.concatenate(split3(jnp.concatenate([merged_lse, own_lse], axis=1)), axis=1)
        parts = jnp.pad(parts, ((0, 0), (0, HD - 3 * each)))[:, None]
        payload = jnp.concatenate(
            [merged.reshape(heads, SLOTS, HD), own, parts, jnp.zeros((heads, 3, HD), BF16)], axis=1
        )
        arrived = a2a(payload, "ctx")

    with jax.named_scope("mix"):
        match = slot[:, None] == jnp.arange(slots, dtype=jnp.int32)[None, :]
        prefix = jnp.dot(
            match.astype(BF16), arrived[:, :SLOTS].reshape(slots, HD), preferred_element_type=F32
        )
        logs = arrived[:, each, : 3 * each].astype(F32).reshape(ctx, 3, each).sum(axis=1)
        prefix_lse = jnp.sum(
            jnp.where(match, logs[:, :SLOTS].reshape(1, slots), 0.0), axis=1, keepdims=True
        )
        own = arrived[:, SLOTS:each].astype(F32).reshape(group_rows, HD)
        own_lse = logs[:, SLOTS:].reshape(group_rows, 1)
        top = jnp.maximum(prefix_lse, own_lse)
        prefix_share = jnp.exp(prefix_lse - top)
        own_share = jnp.exp(own_lse - top)
        attention = (prefix_share * prefix + own_share * own) / (prefix_share + own_share)
        attention = attention.astype(BF16)

    with jax.named_scope("projection"):
        shared = a2a(jnp.broadcast_to(attention[None], (GROUP, *attention.shape)), "ctx", near)
        shared = shared.transpose(1, 0, 2).reshape(group_rows, GROUP * HD)
        terms = lax.dot_general(
            shared, weights, (((1,), (1,)), ((), ())), preferred_element_type=F32
        ).astype(BF16)
        home = a2a(terms.reshape(ctx, rows, -1), "ctx")
        home = home.reshape(ctx // GROUP, GROUP, rows, req, width).astype(F32)
        summed = jnp.sum(home, axis=0).transpose(1, 2, 0, 3)
        return summed.reshape(rows, -1).astype(BF16)


def solution(mesh):
    in_specs = (
        P(("req", "ctx"), None),
        P("req"),
        P(("req", "ctx"), None),
        P("ctx", "req", None),
        P(("req", "ctx"), None, None),
        P("ctx", "req"),
    )
    out_specs = P(("req", "ctx"), None)
    return jax.shard_map(local, mesh=mesh, in_specs=in_specs, out_specs=out_specs, check_vma=False)
```

```python
import functools

import jax
import jax.numpy as jnp
from jax import lax
from jax.experimental import pallas as pl
from jax.experimental.pallas import tpu as pltpu
from jax.sharding import PartitionSpec as P

KVH = 4
HD = 128
SB = 128
SLOTS = 8
GROUP = 8
TILE = 128
FACTOR = HD**-0.5
LOG2E = 1.4426950408889634
NEGATIVE = -1e30
BF16 = jnp.bfloat16
F32 = jnp.float32


def split3(x):
    high = lax.reduce_precision(x, 8, 7)
    rest = x - high
    middle = lax.reduce_precision(rest, 8, 7)
    return high.astype(BF16), middle.astype(BF16), (rest - middle).astype(BF16)


def attention_kernel(q_ref, k_ref, v_ref, out_ref, lse_ref):
    head = pl.program_id(0)
    groups, rows, _ = q_ref.shape
    total = groups * rows
    keys = k_ref[...]
    values = jnp.concatenate([v_ref[...], jnp.ones((v_ref.shape[0], HD), BF16)], axis=1)
    per = TILE // rows

    def score(at):
        queries = q_ref[at * per : (at + 1) * per].reshape(TILE, HD)
        return lax.dot_general(
            queries, keys, (((1,), (1,)), ((), ())), preferred_element_type=F32
        )

    following = score(0)
    for at in range(total // TILE):
        scores = following
        if (at + 1) * TILE < total:
            following = score(at + 1)
        top = jnp.max(scores, axis=1, keepdims=True)
        weights = jnp.exp2((scores - top) * (FACTOR * LOG2E)).astype(BF16)
        both = jnp.dot(weights, values, preferred_element_type=F32)
        summed = both[:, HD:]
        out_ref[at * per : (at + 1) * per, pl.ds(pl.multiple_of(head * rows, rows), rows), :] = (
            (both[:, :HD] / summed).astype(BF16).reshape(per, rows, HD)
        )
        lse = top * FACTOR + jnp.log(summed)
        for j in range(TILE // 128):
            lse_ref[
                pl.ds(pl.multiple_of(head * 8, 8), 8),
                at * TILE + 128 * j : at * TILE + 128 * j + 128,
            ] = lse[128 * j : 128 * j + 128].T[0:8]

    @pl.when(head == KVH - 1)
    def _():
        row = lax.broadcasted_iota(jnp.int32, (8, total), 0)
        upper = jnp.zeros((8, total), F32)
        lower = upper
        for h in range(KVH):
            whole = lse_ref[8 * h : 8 * h + 8, :]
            high = whole.astype(BF16).astype(F32)
            rest = whole - high
            middle = rest.astype(BF16).astype(F32)
            upper = jnp.where(row == h, high, jnp.where(row == KVH + h, middle, upper))
            lower = jnp.where(row == h, rest - middle, lower)
        parts = jnp.concatenate([upper, lower], axis=0)
        rolled = pltpu.roll(parts, total - rows, 1)
        for r in range(groups):
            source = parts if r % 2 == 0 else rolled
            at = r // 2 * 128
            out_ref[r, KVH * rows :, :] = source[:, at : at + 128].astype(BF16)


def prefix_attention(queries, kv):
    groups, rows, _ = queries.shape
    tokens = kv.shape[0]
    each = rows // KVH
    return pl.pallas_call(
        attention_kernel,
        out_shape=jax.ShapeDtypeStruct((groups, rows + 16, HD), BF16),
        grid=(KVH,),
        in_specs=[
            pl.BlockSpec((groups, each, HD), lambda h: (0, h, 0)),
            pl.BlockSpec((tokens, HD), lambda h: (0, h)),
            pl.BlockSpec((tokens, HD), lambda h: (0, KVH + h)),
        ],
        out_specs=pl.BlockSpec((groups, rows + 16, HD), lambda h: (0, 0, 0)),
        scratch_shapes=[pltpu.VMEM((8 * KVH, groups * each), F32)],
        compiler_params=pltpu.CompilerParams(vmem_limit_bytes=48 * 2**20),
        cost_estimate=pl.CostEstimate(
            flops=4 * groups * rows * tokens * HD,
            bytes_accessed=4 * groups * rows * HD + 4 * tokens * KVH * HD,
            transcendentals=groups * rows * tokens,
        ),
    )(queries, kv, kv)


def suffix_attention(query, suffix_kv, lengths):
    rows = query.shape[0]
    positions = suffix_kv.shape[1]
    shaped = query.reshape(rows, KVH, -1, HD)
    keys = suffix_kv[:, :, : KVH * HD].reshape(rows, positions, KVH, HD)
    values = suffix_kv[:, :, KVH * HD :].reshape(rows, positions, KVH, HD)
    scores = jnp.einsum("rkgd,rskd->rkgs", shaped, keys, preferred_element_type=F32) * FACTOR
    live = jnp.arange(positions, dtype=jnp.int32)[None, :] < lengths[:, None]
    scores = jnp.where(live[:, None, None, :], scores, NEGATIVE)
    top = jnp.max(scores, axis=-1, keepdims=True)
    expo = jnp.exp(scores - top)
    summed = jnp.sum(expo, axis=-1, keepdims=True)
    output = (
        jnp.einsum("rkgs,rskd->rkgd", expo.astype(BF16), values, preferred_element_type=F32)
        / summed
    )
    lse = top + jnp.log(summed)
    return output.reshape(rows, -1, HD), lse.reshape(rows, -1, 1)


def a2a(x, axis, groups=None):
    return lax.all_to_all(x, axis, 0, 0, tiled=True, axis_index_groups=groups)


def local(query, prefix_id, suffix_blocks, prefix_kv, suffix_kv, w_out):
    req = lax.axis_size("req")
    ctx = lax.axis_size("ctx")
    rows = query.shape[0]
    heads = query.shape[1] // HD
    group_rows = rows * ctx
    slots = ctx * SLOTS
    near = [list(range(a, a + GROUP)) for a in range(0, ctx, GROUP)]
    far = [list(range(m, ctx, GROUP)) for m in range(GROUP)]
    width = w_out.shape[1] // GROUP
    share = heads // GROUP
    count = heads * SLOTS
    mine = lax.axis_index("ctx") // GROUP

    with jax.named_scope("split_near"):
        asked = query.reshape(rows, GROUP, share, HD).transpose(1, 2, 0, 3)
        asked = asked.reshape(GROUP, share * rows, HD)
        payload = jnp.concatenate([asked, w_out.T.reshape(GROUP, width, HD)], axis=1)
        payload = a2a(payload, "ctx", near)
        asked = payload[:, : share * rows]
        block = payload[:, share * rows :].transpose(1, 0, 2).reshape(width, GROUP * HD)

    with jax.named_scope("weights"):
        weights = a2a(jnp.broadcast_to(block[None], (req, *block.shape)), "req")
        weights = weights.reshape(req * width, GROUP * HD)

    with jax.named_scope("gather_far"):
        asked = lax.all_gather(asked, "ctx", axis=0, tiled=True, axis_index_groups=far)
        asked = asked.reshape(ctx, share, rows, HD).transpose(0, 2, 1, 3)
        asked = asked.reshape(group_rows, share * HD)

    with jax.named_scope("slots"):
        index = jnp.arange(group_rows, dtype=jnp.int32)
        same = prefix_id[:, None] == prefix_id[None, :]
        rank = jnp.sum((same & (index[None, :] < index[:, None])).astype(jnp.int32), axis=1)
        slot = prefix_id * SLOTS + rank
        close = jnp.arange(GROUP * SLOTS, dtype=jnp.int32) + mine * (GROUP * SLOTS)
        place = (slot[None, :] == close[:, None]).astype(BF16)
        picked = jnp.dot(place, asked, preferred_element_type=F32).astype(BF16)
        picked = picked.reshape(GROUP, SLOTS, share, HD).transpose(0, 2, 1, 3)
        picked, weights = lax.optimization_barrier((picked, weights))
        by_slot = a2a(picked, "ctx", near).reshape(count, HD)

    with jax.named_scope("gather_req"):
        spread = jnp.broadcast_to(by_slot[None], (req, *by_slot.shape))
        gathered = a2a(spread, "req")

    with jax.named_scope("prefix"):
        partials = prefix_attention(gathered, prefix_kv[0])
        received = a2a(partials, "req")

    with jax.named_scope("suffix"):
        own, own_lse = suffix_attention(query, suffix_kv, suffix_blocks[0] * SB)
        own = own.astype(BF16).transpose(1, 0, 2)
        own_lse = own_lse[..., 0].T

    with jax.named_scope("merge"):
        logs = received[:, count : count + 3 * KVH, : count // KVH].astype(F32)
        logs = jnp.sum(logs.reshape(req, 3, count), axis=1)
        peak = jnp.max(logs, axis=0)
        shares = jnp.exp(logs - peak)
        total = jnp.sum(shares, axis=0)
        merged = jnp.sum(shares[..., None] * received[:, :count].astype(F32), axis=0)
        merged = (merged / total[:, None]).astype(BF16)
        merged_lse = (peak + jnp.log(total)).reshape(heads, SLOTS)

    with jax.named_scope("to_heads"):
        each = SLOTS + rows
        parts = jnp.concatenate(split3(jnp.concatenate([merged_lse, own_lse], axis=1)), axis=1)
        parts = jnp.pad(parts, ((0, 0), (0, HD - 3 * each)))[:, None]
        payload = jnp.concatenate(
            [merged.reshape(heads, SLOTS, HD), own, parts, jnp.zeros((heads, 3, HD), BF16)], axis=1
        )
        arrived = a2a(payload, "ctx")

    with jax.named_scope("mix"):
        match = slot[:, None] == jnp.arange(slots, dtype=jnp.int32)[None, :]
        prefix = jnp.dot(
            match.astype(BF16), arrived[:, :SLOTS].reshape(slots, HD), preferred_element_type=F32
        )
        logs = arrived[:, each, : 3 * each].astype(F32).reshape(ctx, 3, each).sum(axis=1)
        prefix_lse = jnp.sum(
            jnp.where(match, logs[:, :SLOTS].reshape(1, slots), 0.0), axis=1, keepdims=True
        )
        own = arrived[:, SLOTS:each].astype(F32).reshape(group_rows, HD)
        own_lse = logs[:, SLOTS:].reshape(group_rows, 1)
        top = jnp.maximum(prefix_lse, own_lse)
        prefix_share = jnp.exp(prefix_lse - top)
        own_share = jnp.exp(own_lse - top)
        attention = (prefix_share * prefix + own_share * own) / (prefix_share + own_share)
        attention = attention.astype(BF16)

    with jax.named_scope("projection"):
        shared = a2a(jnp.broadcast_to(attention[None], (GROUP, *attention.shape)), "ctx", near)
        shared = shared.transpose(1, 0, 2).reshape(group_rows, GROUP * HD)
        terms = lax.dot_general(
            shared, weights, (((1,), (1,)), ((), ())), preferred_element_type=F32
        ).astype(BF16)
        home = a2a(terms.reshape(ctx, rows, -1), "ctx")
        home = home.reshape(ctx // GROUP, GROUP, rows, req, width).astype(F32)
        summed = jnp.sum(home, axis=0).transpose(1, 2, 0, 3)
        return summed.reshape(rows, -1).astype(BF16)


def solution(mesh):
    in_specs = (
        P(("req", "ctx"), None),
        P("req"),
        P(("req", "ctx"), None),
        P("ctx", "req", None),
        P(("req", "ctx"), None, None),
        P("ctx", "req"),
    )
    out_specs = P(("req", "ctx"), None)
    return jax.shard_map(local, mesh=mesh, in_specs=in_specs, out_specs=out_specs, check_vma=False)
```

```python
import functools

import jax
import jax.numpy as jnp
from jax import lax
from jax.experimental import pallas as pl
from jax.experimental.pallas import tpu as pltpu
from jax.sharding import PartitionSpec as P

KVH = 4
HD = 128
SB = 128
SLOTS = 8
GROUP = 8
TILE = 128
FACTOR = HD**-0.5
LOG2E = 1.4426950408889634
NEGATIVE = -1e30
BF16 = jnp.bfloat16
F32 = jnp.float32


def split3(x):
    high = lax.reduce_precision(x, 8, 7)
    rest = x - high
    middle = lax.reduce_precision(rest, 8, 7)
    return high.astype(BF16), middle.astype(BF16), (rest - middle).astype(BF16)


def attention_kernel(q_ref, k_ref, v_ref, out_ref, lse_ref):
    head = pl.program_id(0)
    groups, rows, _ = q_ref.shape
    total = groups * rows
    keys = k_ref[...]
    values = jnp.concatenate([v_ref[...], jnp.ones((v_ref.shape[0], HD), BF16)], axis=1)
    per = TILE // rows

    def score(at):
        queries = q_ref[at * per : (at + 1) * per].reshape(TILE, HD)
        return lax.dot_general(
            queries, keys, (((1,), (1,)), ((), ())), preferred_element_type=F32
        )

    following = score(0)
    for at in range(total // TILE):
        scores = following
        if (at + 1) * TILE < total:
            following = score(at + 1)
        top = jnp.max(scores, axis=1, keepdims=True)
        weights = jnp.exp2((scores - top) * (FACTOR * LOG2E)).astype(BF16)
        both = jnp.dot(weights, values, preferred_element_type=F32)
        summed = both[:, HD:]
        out_ref[at * per : (at + 1) * per, pl.ds(pl.multiple_of(head * rows, rows), rows), :] = (
            (both[:, :HD] / summed).astype(BF16).reshape(per, rows, HD)
        )
        lse_ref[pl.ds(pl.multiple_of(head * 8, 8), 8), at * TILE : (at + 1) * TILE] = (
            jnp.broadcast_to(top, (TILE, HD)).T[0:8] * FACTOR + jnp.log(summed.T[0:8])
        )

    @pl.when(head == KVH - 1)
    def _():
        row = lax.broadcasted_iota(jnp.int32, (8, total), 0)
        upper = jnp.zeros((8, total), F32)
        lower = upper
        for h in range(KVH):
            whole = lse_ref[8 * h : 8 * h + 8, :]
            high = whole.astype(BF16).astype(F32)
            rest = whole - high
            middle = rest.astype(BF16).astype(F32)
            upper = jnp.where(row == h, high, jnp.where(row == KVH + h, middle, upper))
            lower = jnp.where(row == h, rest - middle, lower)
        parts = jnp.concatenate([upper, lower], axis=0)
        rolled = pltpu.roll(parts, total - rows, 1)
        for r in range(groups):
            source = parts if r % 2 == 0 else rolled
            at = r // 2 * 128
            out_ref[r, KVH * rows :, :] = source[:, at : at + 128].astype(BF16)


def prefix_attention(queries, kv):
    groups, rows, _ = queries.shape
    tokens = kv.shape[0]
    each = rows // KVH
    return pl.pallas_call(
        attention_kernel,
        out_shape=jax.ShapeDtypeStruct((groups, rows + 16, HD), BF16),
        grid=(KVH,),
        in_specs=[
            pl.BlockSpec((groups, each, HD), lambda h: (0, h, 0)),
            pl.BlockSpec((tokens, HD), lambda h: (0, h)),
            pl.BlockSpec((tokens, HD), lambda h: (0, KVH + h)),
        ],
        out_specs=pl.BlockSpec((groups, rows + 16, HD), lambda h: (0, 0, 0)),
        scratch_shapes=[pltpu.VMEM((8 * KVH, groups * each), F32)],
        compiler_params=pltpu.CompilerParams(vmem_limit_bytes=48 * 2**20),
        cost_estimate=pl.CostEstimate(
            flops=4 * groups * rows * tokens * HD,
            bytes_accessed=4 * groups * rows * HD + 4 * tokens * KVH * HD,
            transcendentals=groups * rows * tokens,
        ),
    )(queries, kv, kv)


def suffix_attention(query, suffix_kv, lengths):
    rows = query.shape[0]
    positions = suffix_kv.shape[1]
    shaped = query.reshape(rows, KVH, -1, HD)
    keys = suffix_kv[:, :, : KVH * HD].reshape(rows, positions, KVH, HD)
    values = suffix_kv[:, :, KVH * HD :].reshape(rows, positions, KVH, HD)
    scores = jnp.einsum("rkgd,rskd->rkgs", shaped, keys, preferred_element_type=F32) * FACTOR
    live = jnp.arange(positions, dtype=jnp.int32)[None, :] < lengths[:, None]
    scores = jnp.where(live[:, None, None, :], scores, NEGATIVE)
    top = jnp.max(scores, axis=-1, keepdims=True)
    expo = jnp.exp(scores - top)
    summed = jnp.sum(expo, axis=-1, keepdims=True)
    output = (
        jnp.einsum("rkgs,rskd->rkgd", expo.astype(BF16), values, preferred_element_type=F32)
        / summed
    )
    lse = top + jnp.log(summed)
    return output.reshape(rows, -1, HD), lse.reshape(rows, -1, 1)


def a2a(x, axis, groups=None):
    return lax.all_to_all(x, axis, 0, 0, tiled=True, axis_index_groups=groups)


def local(query, prefix_id, suffix_blocks, prefix_kv, suffix_kv, w_out):
    req = lax.axis_size("req")
    ctx = lax.axis_size("ctx")
    rows = query.shape[0]
    heads = query.shape[1] // HD
    group_rows = rows * ctx
    slots = ctx * SLOTS
    near = [list(range(a, a + GROUP)) for a in range(0, ctx, GROUP)]
    far = [list(range(m, ctx, GROUP)) for m in range(GROUP)]
    width = w_out.shape[1] // GROUP
    share = heads // GROUP
    count = heads * SLOTS
    mine = lax.axis_index("ctx") // GROUP

    with jax.named_scope("split_near"):
        asked = query.reshape(rows, GROUP, share, HD).transpose(1, 2, 0, 3)
        asked = asked.reshape(GROUP, share * rows, HD)
        payload = jnp.concatenate([asked, w_out.T.reshape(GROUP, width, HD)], axis=1)
        payload = a2a(payload, "ctx", near)
        asked = payload[:, : share * rows]
        block = payload[:, share * rows :].reshape(GROUP // 2, 2, width, HD)
        block = block.transpose(2, 1, 0, 3).reshape(width, GROUP * HD)

    with jax.named_scope("weights"):
        weights = a2a(jnp.broadcast_to(block[None], (req, *block.shape)), "req")
        weights = weights.reshape(req * width, GROUP * HD)

    with jax.named_scope("gather_far"):
        asked = lax.all_gather(asked, "ctx", axis=0, tiled=True, axis_index_groups=far)
        asked = asked.reshape(ctx, share, rows, HD).transpose(0, 2, 1, 3)
        asked = asked.reshape(group_rows, share * HD)

    with jax.named_scope("slots"):
        index = jnp.arange(group_rows, dtype=jnp.int32)
        same = prefix_id[:, None] == prefix_id[None, :]
        rank = jnp.sum((same & (index[None, :] < index[:, None])).astype(jnp.int32), axis=1)
        slot = prefix_id * SLOTS + rank
        close = jnp.arange(GROUP * SLOTS, dtype=jnp.int32) + mine * (GROUP * SLOTS)
        place = (slot[None, :] == close[:, None]).astype(BF16)
        picked = jnp.dot(place, asked, preferred_element_type=F32).astype(BF16)
        picked = picked.reshape(GROUP, SLOTS, share, HD).transpose(0, 2, 1, 3)
        picked, weights = lax.optimization_barrier((picked, weights))
        by_slot = a2a(picked, "ctx", near).reshape(count, HD)

    with jax.named_scope("gather_req"):
        spread = jnp.broadcast_to(by_slot[None], (req, *by_slot.shape))
        gathered = a2a(spread, "req")

    with jax.named_scope("prefix"):
        partials = prefix_attention(gathered, prefix_kv[0])
        received = a2a(partials, "req")

    with jax.named_scope("suffix"):
        own, own_lse = suffix_attention(query, suffix_kv, suffix_blocks[0] * SB)
        own = own.astype(BF16).transpose(1, 0, 2)
        own_lse = own_lse[..., 0].T

    with jax.named_scope("merge"):
        logs = received[:, count : count + 3 * KVH, : count // KVH].astype(F32)
        logs = jnp.sum(logs.reshape(req, 3, count), axis=1)
        peak = jnp.max(logs, axis=0)
        shares = jnp.exp(logs - peak)
        total = jnp.sum(shares, axis=0)
        merged = jnp.sum(shares[..., None] * received[:, :count].astype(F32), axis=0)
        merged = (merged / total[:, None]).astype(BF16)
        merged_lse = (peak + jnp.log(total)).reshape(heads, SLOTS)

    with jax.named_scope("to_heads"):
        each = SLOTS + rows
        parts = jnp.concatenate(split3(jnp.concatenate([merged_lse, own_lse], axis=1)), axis=1)
        parts = jnp.pad(parts, ((0, 0), (0, HD - 3 * each)))[:, None]
        payload = jnp.concatenate(
            [merged.reshape(heads, SLOTS, HD), own, parts, jnp.zeros((heads, 3, HD), BF16)], axis=1
        )
        arrived = a2a(payload, "ctx")

    with jax.named_scope("mix"):
        match = slot[:, None] == jnp.arange(slots, dtype=jnp.int32)[None, :]
        prefix = jnp.dot(
            match.astype(BF16), arrived[:, :SLOTS].reshape(slots, HD), preferred_element_type=F32
        )
        logs = arrived[:, each, : 3 * each].astype(F32).reshape(ctx, 3, each).sum(axis=1)
        prefix_lse = jnp.sum(
            jnp.where(match, logs[:, :SLOTS].reshape(1, slots), 0.0), axis=1, keepdims=True
        )
        own = arrived[:, SLOTS:each].astype(F32).reshape(group_rows, HD)
        own_lse = logs[:, SLOTS:].reshape(group_rows, 1)
        top = jnp.maximum(prefix_lse, own_lse)
        prefix_share = jnp.exp(prefix_lse - top)
        own_share = jnp.exp(own_lse - top)
        attention = (prefix_share * prefix + own_share * own) / (prefix_share + own_share)
        attention = attention.astype(BF16)

    with jax.named_scope("projection"):
        quads = [list(range(a + core, a + GROUP, 2)) for a in range(0, ctx, GROUP) for core in (0, 1)]
        pairs = [[a, a + 1] for a in range(0, ctx, 2)]
        half = GROUP // 2
        shared = a2a(jnp.broadcast_to(attention[None], (half, *attention.shape)), "ctx", quads)
        shared = lax.all_gather(shared, "ctx", axis=0, tiled=True, axis_index_groups=pairs)
        shared = shared.transpose(1, 0, 2).reshape(group_rows, GROUP * HD)
        terms = lax.dot_general(
            shared, weights, (((1,), (1,)), ((), ())), preferred_element_type=F32
        ).astype(BF16)
        home = a2a(terms.reshape(ctx, rows, -1), "ctx")
        home = home.reshape(ctx // GROUP, GROUP, rows, req * width).astype(F32)
        summed = lax.optimization_barrier(jnp.sum(home, axis=0).astype(BF16))
        summed = summed.reshape(GROUP, rows, req, width).transpose(1, 2, 0, 3)
        return summed.reshape(rows, -1)


def solution(mesh):
    in_specs = (
        P(("req", "ctx"), None),
        P("req"),
        P(("req", "ctx"), None),
        P("ctx", "req", None),
        P(("req", "ctx"), None, None),
        P("ctx", "req"),
    )
    out_specs = P(("req", "ctx"), None)
    return jax.shard_map(local, mesh=mesh, in_specs=in_specs, out_specs=out_specs, check_vma=False)
```

```python
import functools

import jax
import jax.numpy as jnp
from jax import lax
from jax.experimental import pallas as pl
from jax.experimental.pallas import tpu as pltpu
from jax.sharding import PartitionSpec as P

KVH = 4
HD = 128
SB = 128
SLOTS = 8
GROUP = 8
TILE = 128
FACTOR = HD**-0.5
LOG2E = 1.4426950408889634
NEGATIVE = -1e30
BF16 = jnp.bfloat16
F32 = jnp.float32


def split3(x):
    high = lax.reduce_precision(x, 8, 7)
    rest = x - high
    middle = lax.reduce_precision(rest, 8, 7)
    return high.astype(BF16), middle.astype(BF16), (rest - middle).astype(BF16)


def attention_kernel(q_ref, kv_ref, out_ref, held, lse_ref, sems):
    groups, all_rows, _ = q_ref.shape
    rows = all_rows // KVH
    total = groups * rows
    per = TILE // rows
    copies = []

    def leave(first, count):
        at = (slice(None), slice(first, first + count))
        copies.append(pltpu.make_async_copy(held.at[at], out_ref.at[at], sems.at[len(copies)]))
        copies[-1].start()

    for head in range(KVH):
        keys = kv_ref[:, head * HD : (head + 1) * HD]
        values = kv_ref[:, (KVH + head) * HD : (KVH + head + 1) * HD]
        values = jnp.concatenate([values, jnp.ones_like(values)], axis=1)
        first = head * rows

        def score(at):
            queries = q_ref[at * per : (at + 1) * per, first : first + rows].reshape(TILE, HD)
            return lax.dot_general(
                queries, keys, (((1,), (1,)), ((), ())), preferred_element_type=F32
            )

        following = score(0)
        for at in range(total // TILE):
            scores = following
            if (at + 1) * TILE < total:
                following = score(at + 1)
            top = jnp.max(scores, axis=1, keepdims=True)
            weights = jnp.exp2((scores - top) * (FACTOR * LOG2E)).astype(BF16)
            both = jnp.dot(weights, values, preferred_element_type=F32)
            summed = both[:, HD:]
            held[at * per : (at + 1) * per, first : first + rows] = (
                (both[:, :HD] / summed).astype(BF16).reshape(per, rows, HD)
            )
            lse_ref[head * 8 : head * 8 + 8, at * TILE : (at + 1) * TILE] = (
                jnp.broadcast_to(top, (TILE, HD)).T[0:8] * FACTOR + jnp.log(summed.T[0:8])
            )
        leave(first, rows)

    row = lax.broadcasted_iota(jnp.int32, (8, total), 0)
    upper = jnp.zeros((8, total), F32)
    lower = upper
    for h in range(KVH):
        whole = lse_ref[8 * h : 8 * h + 8, :]
        high = whole.astype(BF16).astype(F32)
        rest = whole - high
        middle = rest.astype(BF16).astype(F32)
        upper = jnp.where(row == h, high, jnp.where(row == KVH + h, middle, upper))
        lower = jnp.where(row == h, rest - middle, lower)
    parts = jnp.concatenate([upper, lower], axis=0)
    rolled = pltpu.roll(parts, total - rows, 1)
    for r in range(groups):
        source = parts if r % 2 == 0 else rolled
        at = r // 2 * 128
        held[r, all_rows:] = source[:, at : at + 128].astype(BF16)
    leave(all_rows, 16)
    for copy in copies:
        copy.wait()


def prefix_attention(queries, kv):
    groups, rows, _ = queries.shape
    tokens = kv.shape[0]
    return pl.pallas_call(
        attention_kernel,
        out_shape=jax.ShapeDtypeStruct((groups, rows + 16, HD), BF16),
        in_specs=[pl.BlockSpec(memory_space=pltpu.VMEM)] * 2,
        out_specs=pl.BlockSpec(memory_space=pl.ANY),
        scratch_shapes=[
            pltpu.VMEM((groups, rows + 16, HD), BF16),
            pltpu.VMEM((8 * KVH, groups * rows // KVH), F32),
            pltpu.SemaphoreType.DMA((KVH + 1,)),
        ],
        compiler_params=pltpu.CompilerParams(vmem_limit_bytes=40 * 2**20),
        cost_estimate=pl.CostEstimate(
            flops=4 * groups * rows * tokens * HD,
            bytes_accessed=4 * groups * rows * HD + 4 * tokens * KVH * HD,
            transcendentals=groups * rows * tokens,
        ),
    )(queries, kv)


def suffix_attention(query, suffix_kv, lengths):
    rows = query.shape[0]
    positions = suffix_kv.shape[1]
    shaped = query.reshape(rows, KVH, -1, HD)
    keys = suffix_kv[:, :, : KVH * HD].reshape(rows, positions, KVH, HD)
    values = suffix_kv[:, :, KVH * HD :].reshape(rows, positions, KVH, HD)
    scores = jnp.einsum("rkgd,rskd->rkgs", shaped, keys, preferred_element_type=F32) * FACTOR
    live = jnp.arange(positions, dtype=jnp.int32)[None, :] < lengths[:, None]
    scores = jnp.where(live[:, None, None, :], scores, NEGATIVE)
    top = jnp.max(scores, axis=-1, keepdims=True)
    expo = jnp.exp(scores - top)
    summed = jnp.sum(expo, axis=-1, keepdims=True)
    output = (
        jnp.einsum("rkgs,rskd->rkgd", expo.astype(BF16), values, preferred_element_type=F32)
        / summed
    )
    lse = top + jnp.log(summed)
    return output.reshape(rows, -1, HD), lse.reshape(rows, -1, 1)


def a2a(x, axis, groups=None):
    return lax.all_to_all(x, axis, 0, 0, tiled=True, axis_index_groups=groups)


def local(query, prefix_id, suffix_blocks, prefix_kv, suffix_kv, w_out):
    req = lax.axis_size("req")
    ctx = lax.axis_size("ctx")
    rows = query.shape[0]
    heads = query.shape[1] // HD
    group_rows = rows * ctx
    slots = ctx * SLOTS
    near = [list(range(a, a + GROUP)) for a in range(0, ctx, GROUP)]
    far = [list(range(m, ctx, GROUP)) for m in range(GROUP)]
    width = w_out.shape[1] // GROUP
    share = heads // GROUP
    count = heads * SLOTS
    mine = lax.axis_index("ctx") // GROUP

    with jax.named_scope("split_near"):
        asked = query.reshape(rows, GROUP, share, HD).transpose(1, 2, 0, 3)
        asked = asked.reshape(GROUP, share * rows, HD)
        payload = jnp.concatenate([asked, w_out.T.reshape(GROUP, width, HD)], axis=1)
        payload = a2a(payload, "ctx", near)
        asked = payload[:, : share * rows]
        block = payload[:, share * rows :].reshape(GROUP // 2, 2, width, HD)
        block = block.transpose(2, 1, 0, 3).reshape(width, GROUP * HD)

    with jax.named_scope("weights"):
        weights = a2a(jnp.broadcast_to(block[None], (req, *block.shape)), "req")
        weights = weights.reshape(req * width, GROUP * HD)

    with jax.named_scope("gather_far"):
        asked = lax.all_gather(asked, "ctx", axis=0, tiled=True, axis_index_groups=far)
        asked = asked.reshape(ctx, share, rows, HD).transpose(0, 2, 1, 3)
        asked = asked.reshape(group_rows, share * HD)

    with jax.named_scope("slots"):
        index = jnp.arange(group_rows, dtype=jnp.int32)
        same = prefix_id[:, None] == prefix_id[None, :]
        rank = jnp.sum((same & (index[None, :] < index[:, None])).astype(jnp.int32), axis=1)
        slot = prefix_id * SLOTS + rank
        close = jnp.arange(GROUP * SLOTS, dtype=jnp.int32) + mine * (GROUP * SLOTS)
        place = (slot[None, :] == close[:, None]).astype(BF16)
        picked = jnp.dot(place, asked, preferred_element_type=F32).astype(BF16)
        picked = picked.reshape(GROUP, SLOTS, share, HD).transpose(0, 2, 1, 3)
        picked, weights = lax.optimization_barrier((picked, weights))
        by_slot = a2a(picked, "ctx", near).reshape(count, HD)

    with jax.named_scope("gather_req"):
        spread = jnp.broadcast_to(by_slot[None], (req, *by_slot.shape))
        gathered = a2a(spread, "req")

    with jax.named_scope("prefix"):
        partials = prefix_attention(gathered, prefix_kv[0])
        received = a2a(partials, "req")

    with jax.named_scope("suffix"):
        own, own_lse = suffix_attention(query, suffix_kv, suffix_blocks[0] * SB)
        own = own.astype(BF16).transpose(1, 0, 2)
        own_lse = own_lse[..., 0].T

    with jax.named_scope("merge"):
        logs = received[:, count : count + 3 * KVH, : count // KVH].astype(F32)
        logs = jnp.sum(logs.reshape(req, 3, count), axis=1)
        peak = jnp.max(logs, axis=0)
        shares = jnp.exp(logs - peak)
        total = jnp.sum(shares, axis=0)
        merged = jnp.sum(shares[..., None] * received[:, :count].astype(F32), axis=0)
        merged = (merged / total[:, None]).astype(BF16)
        merged_lse = (peak + jnp.log(total)).reshape(heads, SLOTS)

    with jax.named_scope("to_heads"):
        each = SLOTS + rows
        parts = jnp.concatenate(split3(jnp.concatenate([merged_lse, own_lse], axis=1)), axis=1)
        parts = jnp.pad(parts, ((0, 0), (0, HD - 3 * each)))[:, None]
        payload = jnp.concatenate(
            [merged.reshape(heads, SLOTS, HD), own, parts, jnp.zeros((heads, 3, HD), BF16)], axis=1
        )
        arrived = a2a(payload, "ctx")

    with jax.named_scope("mix"):
        match = slot[:, None] == jnp.arange(slots, dtype=jnp.int32)[None, :]
        prefix = jnp.dot(
            match.astype(BF16), arrived[:, :SLOTS].reshape(slots, HD), preferred_element_type=F32
        )
        logs = arrived[:, each, : 3 * each].astype(F32).reshape(ctx, 3, each).sum(axis=1)
        prefix_lse = jnp.sum(
            jnp.where(match, logs[:, :SLOTS].reshape(1, slots), 0.0), axis=1, keepdims=True
        )
        own = arrived[:, SLOTS:each].astype(F32).reshape(group_rows, HD)
        own_lse = logs[:, SLOTS:].reshape(group_rows, 1)
        top = jnp.maximum(prefix_lse, own_lse)
        prefix_share = jnp.exp(prefix_lse - top)
        own_share = jnp.exp(own_lse - top)
        attention = (prefix_share * prefix + own_share * own) / (prefix_share + own_share)
        attention = attention.astype(BF16)

    with jax.named_scope("projection"):
        quads = [list(range(a + core, a + GROUP, 2)) for a in range(0, ctx, GROUP) for core in (0, 1)]
        pairs = [[a, a + 1] for a in range(0, ctx, 2)]
        half = GROUP // 2
        shared = a2a(jnp.broadcast_to(attention[None], (half, *attention.shape)), "ctx", quads)
        shared = lax.all_gather(shared, "ctx", axis=0, tiled=True, axis_index_groups=pairs)
        shared = shared.transpose(1, 0, 2).reshape(group_rows, GROUP * HD)
        terms = lax.dot_general(
            shared, weights, (((1,), (1,)), ((), ())), preferred_element_type=F32
        ).astype(BF16)
        home = a2a(terms.reshape(ctx, rows, -1), "ctx")
        home = home.reshape(ctx // GROUP, GROUP, rows, req * width).astype(F32)
        summed = lax.optimization_barrier(jnp.sum(home, axis=0).astype(BF16))
        summed = summed.reshape(GROUP, rows, req, width).transpose(1, 2, 0, 3)
        return summed.reshape(rows, -1)


def solution(mesh):
    in_specs = (
        P(("req", "ctx"), None),
        P("req"),
        P(("req", "ctx"), None),
        P("ctx", "req", None),
        P(("req", "ctx"), None, None),
        P("ctx", "req"),
    )
    out_specs = P(("req", "ctx"), None)
    return jax.shard_map(local, mesh=mesh, in_specs=in_specs, out_specs=out_specs, check_vma=False)
```

```python
import functools

import jax
import jax.numpy as jnp
from jax import lax
from jax.experimental import pallas as pl
from jax.experimental.pallas import tpu as pltpu
from jax.sharding import PartitionSpec as P

KVH = 4
HD = 128
SB = 128
SLOTS = 8
GROUP = 8
TILE = 128
FACTOR = HD**-0.5
LOG2E = 1.4426950408889634
NEGATIVE = -1e30
BF16 = jnp.bfloat16
F32 = jnp.float32


def split3(x):
    high = lax.reduce_precision(x, 8, 7)
    rest = x - high
    middle = lax.reduce_precision(rest, 8, 7)
    return high.astype(BF16), middle.astype(BF16), (rest - middle).astype(BF16)


def attention_kernel(q_ref, kv_ref, out_ref, held, lse_ref, sems):
    groups, all_rows, _ = q_ref.shape
    rows = all_rows // KVH
    total = groups * rows
    per = TILE // rows
    copies = []

    def leave(first, count):
        at = (slice(None), slice(first, first + count))
        copies.append(pltpu.make_async_copy(held.at[at], out_ref.at[at], sems.at[len(copies)]))
        copies[-1].start()

    for head in range(KVH):
        keys = kv_ref[:, head * HD : (head + 1) * HD]
        values = kv_ref[:, (KVH + head) * HD : (KVH + head + 1) * HD]
        values = jnp.concatenate([values, jnp.ones_like(values)], axis=1)
        first = head * rows

        def score(at):
            queries = q_ref[at * per : (at + 1) * per, first : first + rows].reshape(TILE, HD)
            return lax.dot_general(
                queries, keys, (((1,), (1,)), ((), ())), preferred_element_type=F32
            )

        following = score(0)
        for at in range(total // TILE):
            scores = following
            if (at + 1) * TILE < total:
                following = score(at + 1)
            top = jnp.max(scores, axis=1, keepdims=True)
            weights = jnp.exp2((scores - top) * (FACTOR * LOG2E)).astype(BF16)
            both = jnp.dot(weights, values, preferred_element_type=F32)
            summed = both[:, HD:]
            held[at * per : (at + 1) * per, first : first + rows] = (
                (both[:, :HD] / summed).astype(BF16).reshape(per, rows, HD)
            )
            lse_ref[head * 8 : head * 8 + 8, at * TILE : (at + 1) * TILE] = (
                jnp.broadcast_to(top, (TILE, HD)).T[0:8] * FACTOR + jnp.log(summed.T[0:8])
            )
        leave(first, rows)

    row = lax.broadcasted_iota(jnp.int32, (8, total), 0)
    upper = jnp.zeros((8, total), F32)
    lower = upper
    for h in range(KVH):
        whole = lse_ref[8 * h : 8 * h + 8, :]
        high = whole.astype(BF16).astype(F32)
        rest = whole - high
        middle = rest.astype(BF16).astype(F32)
        upper = jnp.where(row == h, high, jnp.where(row == KVH + h, middle, upper))
        lower = jnp.where(row == h, rest - middle, lower)
    parts = jnp.concatenate([upper, lower], axis=0)
    rolled = pltpu.roll(parts, total - rows, 1)
    for r in range(groups):
        source = parts if r % 2 == 0 else rolled
        at = r // 2 * 128
        held[r, all_rows:] = source[:, at : at + 128].astype(BF16)
    leave(all_rows, 16)
    for copy in copies:
        copy.wait()


def prefix_attention(queries, kv):
    groups, rows, _ = queries.shape
    tokens = kv.shape[0]
    return pl.pallas_call(
        attention_kernel,
        out_shape=jax.ShapeDtypeStruct((groups, rows + 16, HD), BF16),
        in_specs=[pl.BlockSpec(memory_space=pltpu.VMEM)] * 2,
        out_specs=pl.BlockSpec(memory_space=pl.ANY),
        scratch_shapes=[
            pltpu.VMEM((groups, rows + 16, HD), BF16),
            pltpu.VMEM((8 * KVH, groups * rows // KVH), F32),
            pltpu.SemaphoreType.DMA((KVH + 1,)),
        ],
        compiler_params=pltpu.CompilerParams(vmem_limit_bytes=40 * 2**20),
        cost_estimate=pl.CostEstimate(
            flops=4 * groups * rows * tokens * HD,
            bytes_accessed=4 * groups * rows * HD + 4 * tokens * KVH * HD,
            transcendentals=groups * rows * tokens,
        ),
    )(queries, kv)


def suffix_attention(query, suffix_kv, lengths):
    rows = query.shape[0]
    positions = suffix_kv.shape[1]
    shaped = query.reshape(rows, KVH, -1, HD)
    keys = suffix_kv[:, :, : KVH * HD].reshape(rows, positions, KVH, HD)
    values = suffix_kv[:, :, KVH * HD :].reshape(rows, positions, KVH, HD)
    scores = jnp.einsum("rkgd,rskd->rkgs", shaped, keys, preferred_element_type=F32) * FACTOR
    live = jnp.arange(positions, dtype=jnp.int32)[None, :] < lengths[:, None]
    scores = jnp.where(live[:, None, None, :], scores, NEGATIVE)
    top = jnp.max(scores, axis=-1, keepdims=True)
    expo = jnp.exp(scores - top)
    summed = jnp.sum(expo, axis=-1, keepdims=True)
    output = (
        jnp.einsum("rkgs,rskd->rkgd", expo.astype(BF16), values, preferred_element_type=F32)
        / summed
    )
    lse = top + jnp.log(summed)
    return output.reshape(rows, -1, HD), lse.reshape(rows, -1, 1)


def a2a(x, axis, groups=None):
    return lax.all_to_all(x, axis, 0, 0, tiled=True, axis_index_groups=groups)


def local(query, prefix_id, suffix_blocks, prefix_kv, suffix_kv, w_out):
    req = lax.axis_size("req")
    ctx = lax.axis_size("ctx")
    rows = query.shape[0]
    heads = query.shape[1] // HD
    group_rows = rows * ctx
    slots = ctx * SLOTS
    near = [list(range(a, a + GROUP)) for a in range(0, ctx, GROUP)]
    far = [list(range(m, ctx, GROUP)) for m in range(GROUP)]
    width = w_out.shape[1] // GROUP
    share = heads // GROUP
    count = heads * SLOTS
    mine = lax.axis_index("ctx") // GROUP

    with jax.named_scope("split_near"):
        asked = query.reshape(rows, GROUP, share, HD).transpose(1, 2, 0, 3)
        asked = asked.reshape(GROUP, share * rows, HD)
        payload = jnp.concatenate([asked, w_out.T.reshape(GROUP, width, HD)], axis=1)
        payload = a2a(payload, "ctx", near)
        asked = payload[:, : share * rows]
        block = payload[:, share * rows :].reshape(GROUP // 2, 2, width, HD)
        block = block.transpose(2, 1, 0, 3).reshape(width, GROUP * HD)

    with jax.named_scope("weights"):
        weights = a2a(jnp.broadcast_to(block[None], (req, *block.shape)), "req")
        weights = weights.reshape(req * width, GROUP * HD)

    with jax.named_scope("gather_far"):
        asked = lax.all_gather(asked, "ctx", axis=0, tiled=True, axis_index_groups=far)
        asked = asked.reshape(ctx, share, rows, HD).transpose(0, 2, 1, 3)
        asked = asked.reshape(group_rows, share * HD)

    with jax.named_scope("slots"):
        index = jnp.arange(group_rows, dtype=jnp.int32)
        same = prefix_id[:, None] == prefix_id[None, :]
        rank = jnp.sum((same & (index[None, :] < index[:, None])).astype(jnp.int32), axis=1)
        slot = prefix_id * SLOTS + rank
        close = jnp.arange(GROUP * SLOTS, dtype=jnp.int32) + mine * (GROUP * SLOTS)
        place = (slot[None, :] == close[:, None]).astype(BF16)
        picked = jnp.dot(place, asked, preferred_element_type=F32).astype(BF16)
        picked = picked.reshape(GROUP, SLOTS, share, HD).transpose(0, 2, 1, 3)
        picked, weights = lax.optimization_barrier((picked, weights))
        by_slot = a2a(picked, "ctx", near).reshape(count, HD)

    with jax.named_scope("gather_req"):
        spread = jnp.broadcast_to(by_slot[None], (req, *by_slot.shape))
        gathered = a2a(spread, "req")

    with jax.named_scope("prefix"):
        partials = prefix_attention(gathered, prefix_kv[0])
        received = a2a(partials, "req")

    with jax.named_scope("suffix"):
        own, own_lse = suffix_attention(query, suffix_kv, suffix_blocks[0] * SB)
        own = own.astype(BF16).transpose(1, 0, 2)
        own_lse = own_lse[..., 0].T

    with jax.named_scope("merge"):
        logs = received[:, count : count + 3 * KVH, : count // KVH].astype(F32)
        logs = jnp.sum(logs.reshape(req, 3, count), axis=1)
        peak = jnp.max(logs, axis=0)
        shares = jnp.exp(logs - peak)
        total = jnp.sum(shares, axis=0)
        shares = shares / total
        merged = jnp.sum(shares[..., None] * received[:, :count].astype(F32), axis=0)
        merged = merged.astype(BF16)
        merged_lse = (peak + jnp.log(total)).reshape(heads, SLOTS)

    with jax.named_scope("to_heads"):
        each = SLOTS + rows
        parts = jnp.concatenate(split3(jnp.concatenate([merged_lse, own_lse], axis=1)), axis=1)
        parts = jnp.pad(parts, ((0, 0), (0, HD - 3 * each)))[:, None]
        payload = jnp.concatenate(
            [merged.reshape(heads, SLOTS, HD), own, parts, jnp.zeros((heads, 3, HD), BF16)], axis=1
        )
        arrived = a2a(payload, "ctx")

    with jax.named_scope("mix"):
        match = slot[:, None] == jnp.arange(slots, dtype=jnp.int32)[None, :]
        prefix = jnp.dot(
            match.astype(BF16), arrived[:, :SLOTS].reshape(slots, HD), preferred_element_type=F32
        )
        logs = arrived[:, each, : 3 * each].astype(F32).reshape(ctx, 3, each).sum(axis=1)
        prefix_lse = jnp.sum(
            jnp.where(match, logs[:, :SLOTS].reshape(1, slots), 0.0), axis=1, keepdims=True
        )
        own = arrived[:, SLOTS:each].astype(F32).reshape(group_rows, HD)
        own_lse = logs[:, SLOTS:].reshape(group_rows, 1)
        top = jnp.maximum(prefix_lse, own_lse)
        prefix_share = jnp.exp(prefix_lse - top)
        own_share = jnp.exp(own_lse - top)
        attention = (prefix_share * prefix + own_share * own) / (prefix_share + own_share)
        attention = attention.astype(BF16)

    with jax.named_scope("projection"):
        quads = [list(range(a + core, a + GROUP, 2)) for a in range(0, ctx, GROUP) for core in (0, 1)]
        pairs = [[a, a + 1] for a in range(0, ctx, 2)]
        half = GROUP // 2
        shared = a2a(jnp.broadcast_to(attention[None], (half, *attention.shape)), "ctx", quads)
        shared = lax.all_gather(shared, "ctx", axis=0, tiled=True, axis_index_groups=pairs)
        shared = shared.transpose(1, 0, 2).reshape(group_rows, GROUP * HD)
        terms = lax.dot_general(
            shared, weights, (((1,), (1,)), ((), ())), preferred_element_type=F32
        ).astype(BF16)
        home = a2a(terms.reshape(ctx, rows, -1), "ctx")
        home = home.reshape(ctx // GROUP, GROUP, rows, req * width).astype(F32)
        summed = lax.optimization_barrier(jnp.sum(home, axis=0).astype(BF16))
        summed = summed.reshape(GROUP, rows, req, width).transpose(1, 2, 0, 3)
        return summed.reshape(rows, -1)


def solution(mesh):
    in_specs = (
        P(("req", "ctx"), None),
        P("req"),
        P(("req", "ctx"), None),
        P("ctx", "req", None),
        P(("req", "ctx"), None, None),
        P("ctx", "req"),
    )
    out_specs = P(("req", "ctx"), None)
    return jax.shard_map(local, mesh=mesh, in_specs=in_specs, out_specs=out_specs, check_vma=False)
```
